32 devices in a mesh: row: 4 (over x, core), col: 2 (over y), layer: 4 (over z).
Axes of the slice: x: 2, y: 2, z: 4, core: 2. Of those that a mesh axis runs over, the one named last changes fastest.
Arguments:
- matrix_values: float32 [4, 1024, 4, 1024], P(None, 'row', 'layer', 'col'), may hold values from 4.8828125e-08 to 1.2001953
- matrix_pattern: int32 [4, 4, 4, 4], P(None, 'row', 'layer', 'col'), may hold values from 0 to 1, as said below
- panel: float32 [4, 1024, 1024], P('layer', 'row', 'col'), may hold values from 0.0009 to 1097
- panel_pattern: int32 [4, 4, 4], P('layer', 'row', 'col'), may hold values from 0 to 1, as said below
- out_pattern: int32 [4, 4, 4], P('layer', 'row', 'col'), may hold values from 0 to 1, as said below
Outputs:
- inflated: float32 [4, 1024, 1024], P('layer', 'row', 'col')
The draws below stay inside these ranges and needn't reach their ends.
Inputs may be any that keep to these rules, and one draw needn't show every extreme that they name: `matrix_pattern`: every tile on the diagonal of the 4096 x 4096 matrix is present. `panel_pattern`: for every column tile, some row tile is present both here and in out_pattern. `out_pattern`: for every column tile, some row tile is present both here and in panel_pattern.
All inputs are finite; a program needn't handle non-finite values.
Results may differ from the reference program's by a relative error of at most 0.0001.
Values sent between devices are 32-bit elements; how exact they have to be, the bound alone decides.
A program may use at most 64 MiB of HBM per device.

```python
import jax
import jax.numpy as jnp
from jax import lax

TILE = 256
PRODUCTS = 2
KL = 1024
NM = 4096
W = 1024
N_LAYER = 4


def forced_tiles(key):
    return jax.random.randint(jax.random.fold_in(key, 101), (W // TILE,), 0, NM // TILE)


def index_factors(key, row_spread, column_spread):
    row_factor = jnp.exp(jax.random.uniform(jax.random.fold_in(key, 201), (NM,), jnp.float32, -row_spread, row_spread))
    column_factor = jnp.exp(jax.random.uniform(jax.random.fold_in(key, 202), (NM,), jnp.float32, -column_spread, column_spread))
    return (row_factor, column_factor)


def draw_matrix_values(key, part):
    shape = (N_LAYER, KL, N_LAYER, KL)
    row_factor, column_factor = index_factors(key, 1.5, 2.5)
    key = jax.random.fold_in(key, 11)
    base = jnp.exp(jax.random.truncated_normal(key, -3.0, 3.0, shape, jnp.float32))
    rows = row_factor.reshape(N_LAYER, KL, 1, 1)
    inner = (column_factor / row_factor).reshape(1, 1, N_LAYER, KL)
    return (base * rows * inner / NM).astype(jnp.float32)


def draw_panel(key, part):
    shape = (N_LAYER, KL, W)
    row_factor, column_factor = index_factors(key, 1.5, 2.5)
    key = jax.random.fold_in(key, 13)
    base = jnp.exp(jax.random.truncated_normal(key, -3.0, 3.0, shape, jnp.float32))
    rows = (row_factor / column_factor).reshape(N_LAYER, KL, 1)
    return (base * rows).astype(jnp.float32)


def draw_matrix_pattern(key, part):
    key = jax.random.fold_in(key, 3)
    tiles = KL // TILE
    level = jax.random.randint(jax.random.fold_in(key, 1), (N_LAYER, tiles, 1, 1), 15, 90)
    roll = jax.random.randint(jax.random.fold_in(key, 2), (N_LAYER, tiles, N_LAYER, tiles), 0, 100)
    first = jnp.arange(N_LAYER)[:, None, None, None]
    second = jnp.arange(tiles)[None, :, None, None]
    third = jnp.arange(N_LAYER)[None, None, :, None]
    fourth = jnp.arange(tiles)[None, None, None, :]
    diagonal = (first == third) & (second == fourth)
    return jnp.where(diagonal | (roll < level), 1, 0).astype(jnp.int32)


def column_pattern(key, salt, percent):
    forced = forced_tiles(key)
    key = jax.random.fold_in(key, salt)
    tiles = KL // TILE
    roll = jax.random.randint(key, (N_LAYER, tiles, W // TILE), 0, 100)
    global_row = jnp.arange(N_LAYER)[:, None, None] * tiles + jnp.arange(tiles)[None, :, None]
    chosen = global_row == forced[None, None, :]
    return jnp.where(chosen | (roll < percent), 1, 0).astype(jnp.int32)


def draw_panel_pattern(key, part):
    return column_pattern(key, 5, 50)


def draw_out_pattern(key, part):
    return column_pattern(key, 7, 40)


def setup_inputs(seed: int = 0) -> dict:
    keys = jax.random.split(jax.random.key(seed), 6)
    return {
        "matrix_values": draw_matrix_values(jax.random.fold_in(keys[5], 71), 0),
        "matrix_pattern": draw_matrix_pattern(jax.random.fold_in(keys[5], 71), 0),
        "panel": draw_panel(jax.random.fold_in(keys[5], 71), 0),
        "panel_pattern": draw_panel_pattern(jax.random.fold_in(keys[5], 71), 0),
        "out_pattern": draw_out_pattern(jax.random.fold_in(keys[5], 71), 0),
    }


def spread(pattern, dimensions, tile):
    grown = pattern.astype(jnp.float32)
    for dimension in dimensions:
        grown = jnp.repeat(grown, tile, axis=dimension)
    return grown


def reference(matrix_values, matrix_pattern, panel, panel_pattern, out_pattern):
    tile = matrix_values.shape[1] // matrix_pattern.shape[1]
    order = matrix_values.shape[0] * matrix_values.shape[1]
    live_matrix = (matrix_values * spread(matrix_pattern, (1, 3), tile)).reshape(order, order)
    current = (panel * spread(panel_pattern, (1, 2), tile)).reshape(order, panel.shape[2])
    for stepnum in range(PRODUCTS):
        current = jnp.dot(live_matrix, current, precision=lax.Precision.HIGHEST, preferred_element_type=jnp.float32)
    kept_cells = spread(out_pattern, (1, 2), tile).reshape(order, panel.shape[2])
    squared = current * current * kept_cells
    column_total = jnp.sum(squared, axis=0)
    kept = jnp.sum(kept_cells, axis=0)
    return (squared * (kept / column_total)[None, :]).reshape(panel.shape)
```

```python
import functools

import jax
import jax.numpy as jnp
from jax import lax
from jax.experimental import pallas as pl
from jax.experimental.pallas import tpu as pltpu
from jax.sharding import PartitionSpec as P

TILE = 256
MESH = pl.DeviceIdType.MESH
ROW_CHUNKS = 2
COLUMN_CHUNKS = 4
F32 = jnp.float32
BF16 = jnp.bfloat16


def slab_order(layers):
    table = []
    for layer in range(layers):
        up = list(range(layers - 1, layer, -1))
        down = list(range(layer))
        first, second = (up, down) if len(up) >= len(down) else (down, up)
        order = []
        for i in range(len(first)):
            order.append(first[i])
            if i < len(second):
                order.append(second[i])
        table.append(order + [layer])
    return table


def split(value):
    high = value.astype(BF16)
    return high, (value - high.astype(F32)).astype(BF16)


def kernel(
    sizes, mp, pp, op, a_ref, x_ref, sq_ref, tot_ref,
    a_send, a_recv, ah, al, xg, xh, xl, zs1, zr1, zs2, zr2, tz, tr,
    a_ss, a_rs, x_ss, x_fs, x_rs, z1_ss, z1_rs, z2_ss, z2_rs, tz_ss, tz_rs, tr_ss, tr_rs,
):
    n_row, n_col, n_layer = sizes
    slabs, rows, depth = a_ref.shape
    width = x_ref.shape[1]
    rc = rows // ROW_CHUNKS
    wc = width // COLUMN_CHUNKS
    row_tiles, depth_tiles, width_tiles = rows // TILE, depth // TILE, width // TILE
    r, c, l = lax.axis_index("row"), lax.axis_index("col"), lax.axis_index("layer")
    sibling = r + 1 - 2 * lax.rem(r, 2)
    n_x = n_row // 2
    table = slab_order(n_layer)

    def order(s):
        index = l * n_layer + s
        a = jnp.int32(0)
        for i in range(n_layer):
            for j in range(n_layer):
                if table[i][j]:
                    a = jnp.where(index == i * n_layer + j, table[i][j], a)
        return a

    def remote(src, dst, ss, rs, **device):
        return pltpu.make_async_remote_copy(
            src_ref=src, dst_ref=dst, send_sem=ss, recv_sem=rs, device_id=device, device_id_type=MESH
        )

    barrier = pltpu.get_barrier_semaphore()
    for o in range(1, n_col):
        pl.semaphore_signal(barrier, inc=1, device_id={"col": lax.rem(c + o, n_col)}, device_id_type=MESH)
    for o in range(1, n_row):
        pl.semaphore_signal(barrier, inc=1, device_id={"row": lax.rem(r + o, n_row)}, device_id_type=MESH)
    for o in range(1, n_layer):
        pl.semaphore_signal(barrier, inc=1, device_id={"layer": lax.rem(l + o, n_layer)}, device_id_type=MESH)

    def x_copies(step, j):
        own = xg.at[step, r, j]
        yield remote(own, own, x_ss.at[step, j, 0], x_rs.at[step, j, r], row=sibling)
        for o in range(1, n_x):
            yield remote(own, own, x_ss.at[step, j, o], x_rs.at[step, j, r], row=lax.rem(r + 2 * o, n_row))

    def x_forward(step, j, o):
        source = lax.rem(r + n_row - 2 * o, n_row)
        block = xg.at[step, source, j]
        return remote(block, block, x_fs.at[step, j, o - 1], x_rs.at[step, j, source], row=sibling)

    def forward(step, j):
        for o in range(1, n_x):
            copy = x_forward(step, j, o)
            copy.wait_recv()
            copy.start()

    def finish(step, j):
        for o in range(n_x):
            source = lax.rem(sibling + n_row - 2 * o, n_row)
            block = xg.at[step, source, j]
            remote(block, block, x_ss.at[step, j, 0], x_rs.at[step, j, source], row=sibling).wait_recv()
        columns = pl.ds(pl.multiple_of(j * wc, wc), wc)
        for source in range(n_row):
            high, low = split(xg[step, source, j])
            xh[source * rows:(source + 1) * rows, columns] = high
            xl[source * rows:(source + 1) * rows, columns] = low

    def a_copy(o, s, h):
        a = order(s)
        part = pl.ds(pl.multiple_of(h * rc, rc), rc)
        return remote(
            a_send.at[a, part, :], a_recv.at[o - 1, a, part, :], a_ss.at[o - 1, s, h], a_rs.at[o - 1, s, h],
            col=lax.rem(c + o, n_col),
        )

    def keep_a(source, a, part, value):
        columns = pl.ds(pl.multiple_of(source * depth, depth), depth)
        high, low = split(value)
        ah[a, part, columns] = high
        al[a, part, columns] = low

    def product(a, part, columns):
        high = ah[a, part, :]
        right = xh[:, columns]
        total = jnp.dot(high, right, preferred_element_type=F32)
        total += jnp.dot(high, xl[:, columns], preferred_element_type=F32)
        return total + jnp.dot(al[a, part, :], right, preferred_element_type=F32)

    def pass_on(zs, zr, ss, rs, a, s, j):
        upward = a > l
        slot = jnp.where(a == l - 1, n_layer, a)
        target = jnp.where(upward, l + 1, l - 1)

        @pl.when(jnp.where(upward, l, n_layer - 1 - l) > 0)
        def _():
            remote(zs.at[s, j], zr.at[a, j], ss.at[s, j], rs.at[a, j], layer=target).wait_recv()
            zs[s, j] += zr[a, j]

        remote(zs.at[s, j], zr.at[slot, j], ss.at[s, j], rs.at[slot, j], layer=target).start()

    def receive_own(zs, zr, ss, rs, j):
        last = n_layer - 1

        @pl.when(l > 0)
        def _():
            remote(zs.at[last, j], zr.at[l, j], ss.at[0, j], rs.at[l, j], layer=l - 1).wait_recv()
            zs[last, j] += zr[l, j]

        @pl.when(l < last)
        def _():
            remote(zs.at[last, j], zr.at[n_layer, j], ss.at[0, j], rs.at[n_layer, j], layer=l + 1).wait_recv()
            zs[last, j] += zr[n_layer, j]

    def loop(count, body):
        lax.fori_loop(0, count, lambda i, carry: (body(i), carry)[1], 0)

    def mask_x(j):
        tile = (j * wc) // TILE
        for t in range(row_tiles):
            keep = pp[t * width_tiles + tile].astype(F32)
            xg[0, r, j, t * TILE:(t + 1) * TILE, :] = (
                x_ref[t * TILE:(t + 1) * TILE, pl.ds(pl.multiple_of(j * wc, wc), wc)] * keep
            )

    def mask_a(s, h):
        a = order(s)
        part = pl.ds(pl.multiple_of(h * rc, rc), rc)
        for t in range(depth_tiles):
            keep = mp[(a * row_tiles + (h * rc) // TILE) * depth_tiles + t].astype(F32)
            a_send[a, part, t * TILE:(t + 1) * TILE] = a_ref[a, part, t * TILE:(t + 1) * TILE] * keep

    mask_a(0, 0)
    loop(COLUMN_CHUNKS, mask_x)
    pl.semaphore_wait(barrier, n_col + n_row + n_layer - 3)

    def send_a(s, h):
        for o in range(1, n_col):
            a_copy(o, s, h).start()

    def send_x(step):
        def body(j):
            for copy in x_copies(step, j):
                copy.start()
        loop(COLUMN_CHUNKS, body)

    send_a(0, 0)
    send_x(0)

    def start_a(u):
        s, h = u // ROW_CHUNKS, u % ROW_CHUNKS

        @pl.when(u > 0)
        def _():
            mask_a(s, h)
            send_a(s, h)

    loop(n_layer * ROW_CHUNKS, start_a)

    def own_a(u):
        s, h = u // ROW_CHUNKS, u % ROW_CHUNKS
        a = order(s)
        part = pl.ds(pl.multiple_of(h * rc, rc), rc)
        keep_a(c, a, part, a_send[a, part, :])

    loop(n_layer * ROW_CHUNKS, own_a)
    loop(COLUMN_CHUNKS, lambda j: forward(0, j))
    loop(COLUMN_CHUNKS, lambda j: finish(0, j))

    def first(s, h):
        a = order(s)
        part = pl.ds(pl.multiple_of(h * rc, rc), rc)
        for o in range(1, n_col):
            a_copy(o, s, h).wait_recv()
            keep_a(lax.rem(c + n_col - o, n_col), a, part, a_recv[o - 1, a, part, :])
        zs1[s, h] = product(a, part, pl.ds(0, width))
        return a, part

    def first_others(u):
        s, h = u // ROW_CHUNKS, u % ROW_CHUNKS
        a, part = first(s, h)
        pass_on(zs1, zr1, z1_ss, z1_rs, a, s, h)

    loop((n_layer - 1) * ROW_CHUNKS, first_others)

    def first_own(h):
        a, part = first(n_layer - 1, h)
        receive_own(zs1, zr1, z1_ss, z1_rs, h)
        for j in range(COLUMN_CHUNKS):
            xg[1, r, j, part, :] = zs1[n_layer - 1, h, :, j * wc:(j + 1) * wc]

    loop(ROW_CHUNKS, first_own)

    send_x(1)
    whole = pl.ds(0, rows)

    def others(j):
        columns = pl.ds(pl.multiple_of(j * wc, wc), wc)
        finish(1, j)

        def each(s):
            a = order(s)
            zs2[s, j] = product(a, whole, columns)
            pass_on(zs2, zr2, z2_ss, z2_rs, a, s, j)

        loop(n_layer - 1, each)

    def own(j):
        columns = pl.ds(pl.multiple_of(j * wc, wc), wc)
        zs2[n_layer - 1, j] = product(l, whole, columns)
        receive_own(zs2, zr2, z2_ss, z2_rs, j)
        tile = (j * wc) // TILE
        total = jnp.zeros((1, wc), F32)
        kept = jnp.zeros((1, wc), F32)
        for t in range(row_tiles):
            keep = op[t * width_tiles + tile].astype(F32)
            value = zs2[n_layer - 1, j, t * TILE:(t + 1) * TILE, :]
            squared = value * value * keep
            sq_ref[t * TILE:(t + 1) * TILE, columns] = squared
            total += jnp.sum(squared, axis=0, keepdims=True)
            kept += keep * TILE
        tz[l, 0:1, columns] = total
        tz[l, 1:2, columns] = kept

    tz[l] = jnp.zeros_like(tz[l])
    forward(1, 0)

    def second(j):
        @pl.when(j < COLUMN_CHUNKS)
        def _():
            others(j)

        @pl.when(j < COLUMN_CHUNKS - 1)
        def _():
            forward(1, j + 1)

        @pl.when(j > 0)
        def _():
            own(j - 1)

    loop(COLUMN_CHUNKS + 1, second)

    def tz_copy(o):
        return remote(tz.at[l], tz.at[l], tz_ss.at[o - 1], tz_rs.at[o - 1], layer=lax.rem(l + o, n_layer))

    def tr_copy(o):
        return remote(tr.at[r], tr.at[r], tr_ss.at[o - 1], tr_rs.at[o - 1], row=lax.rem(r + o, n_row))

    for o in range(1, n_layer):
        tz_copy(o).start()
    for o in range(1, n_layer):
        source = lax.rem(l + n_layer - o, n_layer)
        remote(tz.at[l], tz.at[source], tz_ss.at[o - 1], tz_rs.at[o - 1], layer=source).wait_recv()
    tr[r] = sum(tz[i] for i in range(n_layer))
    for o in range(1, n_row):
        tr_copy(o).start()
    for o in range(1, n_row):
        source = lax.rem(r + n_row - o, n_row)
        remote(tr.at[r], tr.at[source], tr_ss.at[o - 1], tr_rs.at[o - 1], row=source).wait_recv()
    tot_ref[...] = sum(tr[i] for i in range(n_row))

    def a_left(u):
        s, h = u // ROW_CHUNKS, u % ROW_CHUNKS
        for o in range(1, n_col):
            a_copy(o, s, h).wait_send()

    loop(n_layer * ROW_CHUNKS, a_left)

    def z1_left(u):
        s, h = u // ROW_CHUNKS, u % ROW_CHUNKS
        block = zs1.at[s, h]
        remote(block, block, z1_ss.at[s, h], z1_rs.at[0, h], layer=lax.rem(l + 1, n_layer)).wait_send()

    loop((n_layer - 1) * ROW_CHUNKS, z1_left)

    def chunk_left(j):
        for step in range(2):
            for copy in x_copies(step, j):
                copy.wait_send()
            for o in range(1, n_x):
                x_forward(step, j, o).wait_send()
        for s in range(n_layer - 1):
            block = zs2.at[s, j]
            remote(block, block, z2_ss.at[s, j], z2_rs.at[0, j], layer=lax.rem(l + 1, n_layer)).wait_send()

    loop(COLUMN_CHUNKS, chunk_left)
    for o in range(1, n_layer):
        tz_copy(o).wait_send()
    for o in range(1, n_row):
        tr_copy(o).wait_send()


def body(sizes, matrix_values, matrix_pattern, panel, panel_pattern, out_pattern):
    n_row, n_col, n_layer = sizes
    slabs, rows, _, depth = matrix_values.shape
    width = panel.shape[2]
    inner = depth * n_col
    rc, wc = rows // ROW_CHUNKS, width // COLUMN_CHUNKS
    n_x = n_row // 2
    dma = pltpu.SemaphoreType.DMA
    squared, totals = pl.pallas_call(
        functools.partial(kernel, sizes),
        out_shape=(
            jax.ShapeDtypeStruct((rows, width), F32),
            jax.ShapeDtypeStruct((8, width), F32),
        ),
        in_specs=[pl.BlockSpec(memory_space=pltpu.SMEM)] * 3 + [pl.BlockSpec(memory_space=pltpu.VMEM)] * 2,
        out_specs=(pl.BlockSpec(memory_space=pltpu.VMEM),) * 2,
        scratch_shapes=[
            pltpu.VMEM((slabs, rows, depth), F32),
            pltpu.VMEM((n_col - 1, slabs, rows, depth), F32),
            pltpu.VMEM((slabs, rows, inner), BF16),
            pltpu.VMEM((slabs, rows, inner), BF16),
            pltpu.VMEM((2, n_row, COLUMN_CHUNKS, rows, wc), F32),
            pltpu.VMEM((inner, width), BF16),
            pltpu.VMEM((inner, width), BF16),
            pltpu.VMEM((n_layer, ROW_CHUNKS, rc, width), F32),
            pltpu.VMEM((n_layer + 1, ROW_CHUNKS, rc, width), F32),
            pltpu.VMEM((n_layer, COLUMN_CHUNKS, rows, wc), F32),
            pltpu.VMEM((n_layer + 1, COLUMN_CHUNKS, rows, wc), F32),
            pltpu.VMEM((n_layer, 8, width), F32),
            pltpu.VMEM((n_row, 8, width), F32),
            dma((n_col - 1, n_layer, ROW_CHUNKS)),
            dma((n_col - 1, n_layer, ROW_CHUNKS)),
            dma((2, COLUMN_CHUNKS, n_x)),
            dma((2, COLUMN_CHUNKS, n_x)),
            dma((2, COLUMN_CHUNKS, n_row)),
            dma((n_layer, ROW_CHUNKS)),
            dma((n_layer + 1, ROW_CHUNKS)),
            dma((n_layer, COLUMN_CHUNKS)),
            dma((n_layer + 1, COLUMN_CHUNKS)),
            dma((n_layer - 1,)),
            dma((n_layer - 1,)),
            dma((n_row - 1,)),
            dma((n_row - 1,)),
        ],
        compiler_params=pltpu.CompilerParams(
            collective_id=0, has_side_effects=True, vmem_limit_bytes=56 * 1024 * 1024
        ),
        name="walk",
    )(
        matrix_pattern.reshape(-1),
        panel_pattern.reshape(-1),
        out_pattern.reshape(-1),
        matrix_values.reshape(slabs, rows, depth),
        panel.reshape(rows, width),
    )
    return (squared * (totals[1] / totals[0])[None, :])[None]


def solution(mesh):
    placed = (
        P(None, "row", "layer", "col"),
        P(None, "row", "layer", "col"),
        P("layer", "row", "col"),
        P("layer", "row", "col"),
        P("layer", "row", "col"),
    )
    sizes = (mesh.shape["row"], mesh.shape["col"], mesh.shape["layer"])
    return jax.shard_map(
        functools.partial(body, sizes), mesh=mesh, in_specs=placed, out_specs=P("layer", "row", "col"),
        check_vma=False,
    )
```

```python
import functools

import jax
import jax.numpy as jnp
from jax import lax
from jax.experimental import pallas as pl
from jax.experimental.pallas import tpu as pltpu
from jax.sharding import PartitionSpec as P

TILE = 256
MESH = pl.DeviceIdType.MESH
ROW_CHUNKS = 2
COLUMN_CHUNKS = 4
F32 = jnp.float32
BF16 = jnp.bfloat16


def slab_order(layers):
    table = []
    for layer in range(layers):
        up = list(range(layers - 1, layer, -1))
        down = list(range(layer))
        first, second = (up, down) if len(up) >= len(down) else (down, up)
        order = []
        for i in range(len(first)):
            order.append(first[i])
            if i < len(second):
                order.append(second[i])
        table.append(order + [layer])
    return table


def split(value):
    high = value.astype(BF16)
    return high, (value - high.astype(F32)).astype(BF16)


def kernel(
    sizes, mp, pp, op, a_hbm, x_ref, sq_ref, fac_ref,
    a_ref, a_send, a_recv, ah, al, xg, xh, xl, zs1, zr1, zs2, zr2, tots,
    a_ls, a_ss, a_rs, x_ss, x_fs, x_rs, z1_ss, z1_rs, z2_ss, z2_rs, t_ss, t_rs,
):
    n_row, n_col, n_layer = sizes
    slabs, rows, depth = a_ref.shape
    width = x_ref.shape[1]
    rc = rows // ROW_CHUNKS
    wc = width // COLUMN_CHUNKS
    row_tiles, depth_tiles, width_tiles = rows // TILE, depth // TILE, width // TILE
    r, c, l = lax.axis_index("row"), lax.axis_index("col"), lax.axis_index("layer")
    sibling = r + 1 - 2 * lax.rem(r, 2)
    n_x = n_row // 2
    table = slab_order(n_layer)

    def order(s):
        index = l * n_layer + s
        a = jnp.int32(0)
        for i in range(n_layer):
            for j in range(n_layer):
                if table[i][j]:
                    a = jnp.where(index == i * n_layer + j, table[i][j], a)
        return a

    def remote(src, dst, ss, rs, **device):
        return pltpu.make_async_remote_copy(
            src_ref=src, dst_ref=dst, send_sem=ss, recv_sem=rs, device_id=device, device_id_type=MESH
        )

    barrier = pltpu.get_barrier_semaphore()
    for o in range(1, n_col):
        pl.semaphore_signal(barrier, inc=1, device_id={"col": lax.rem(c + o, n_col)}, device_id_type=MESH)
    for o in range(1, n_row * n_layer):
        to_row, to_layer = lax.rem(r + o // n_layer, n_row), lax.rem(l + o % n_layer, n_layer)
        pl.semaphore_signal(barrier, inc=1, device_id={"row": to_row, "layer": to_layer}, device_id_type=MESH)

    def load_a(s, h):
        a = order(s)
        part = pl.ds(pl.multiple_of(h * rc, rc), rc)
        return pltpu.make_async_copy(a_hbm.at[a, part, 0, :], a_ref.at[a, part, :], a_ls.at[s, h])

    def x_block(step, source, j, h):
        return xg.at[step, source, j, pl.ds(pl.multiple_of(h * rc, rc), rc), :]

    def x_copies(step, j, h):
        own = x_block(step, r, j, h)
        yield remote(own, own, x_ss.at[step, j, h, 0], x_rs.at[step, j, h, r], row=sibling)
        for o in range(1, n_x):
            yield remote(own, own, x_ss.at[step, j, h, o], x_rs.at[step, j, h, r], row=lax.rem(r + 2 * o, n_row))

    def x_forward(step, j, h, o):
        source = lax.rem(r + n_row - 2 * o, n_row)
        block = x_block(step, source, j, h)
        return remote(block, block, x_fs.at[step, j, h, o - 1], x_rs.at[step, j, h, source], row=sibling)

    def forward(step, j):
        for h in range(ROW_CHUNKS):
            for o in range(1, n_x):
                copy = x_forward(step, j, h, o)
                copy.wait_recv()
                copy.start()

    def finish(step, j):
        for h in range(ROW_CHUNKS):
            for o in range(n_x):
                source = lax.rem(sibling + n_row - 2 * o, n_row)
                block = x_block(step, source, j, h)
                remote(block, block, x_ss.at[step, j, h, 0], x_rs.at[step, j, h, source], row=sibling).wait_recv()
        columns = pl.ds(pl.multiple_of(j * wc, wc), wc)
        for source in range(n_row):
            high, low = split(xg[step, source, j])
            xh[source * rows:(source + 1) * rows, columns] = high
            xl[source * rows:(source + 1) * rows, columns] = low

    def a_copy(o, s, h):
        a = order(s)
        part = pl.ds(pl.multiple_of(h * rc, rc), rc)
        return remote(
            a_send.at[a, part, :], a_recv.at[o - 1, a, part, :], a_ss.at[o - 1, s, h], a_rs.at[o - 1, s, h],
            col=lax.rem(c + o, n_col),
        )

    def keep_a(source, a, part, value):
        columns = pl.ds(pl.multiple_of(source * depth, depth), depth)
        high, low = split(value)
        ah[a, part, columns] = high
        al[a, part, columns] = low

    def product(a, part, columns):
        high = ah[a, part, :]
        right = xh[:, columns]
        total = jnp.dot(high, right, preferred_element_type=F32)
        total += jnp.dot(high, xl[:, columns], preferred_element_type=F32)
        return total + jnp.dot(al[a, part, :], right, preferred_element_type=F32)

    def pass_on(zs, zr, ss, rs, a, s, j):
        upward = a > l
        slot = jnp.where(a == l - 1, n_layer, a)
        target = jnp.where(upward, l + 1, l - 1)

        @pl.when(jnp.where(upward, l, n_layer - 1 - l) > 0)
        def _():
            remote(zs.at[s, j], zr.at[a, j], ss.at[s, j], rs.at[a, j], layer=target).wait_recv()
            zs[s, j] += zr[a, j]

        remote(zs.at[s, j], zr.at[slot, j], ss.at[s, j], rs.at[slot, j], layer=target).start()

    def receive_own(zs, zr, ss, rs, j):
        last = n_layer - 1

        @pl.when(l > 0)
        def _():
            remote(zs.at[last, j], zr.at[l, j], ss.at[0, j], rs.at[l, j], layer=l - 1).wait_recv()
            zs[last, j] += zr[l, j]

        @pl.when(l < last)
        def _():
            remote(zs.at[last, j], zr.at[n_layer, j], ss.at[0, j], rs.at[n_layer, j], layer=l + 1).wait_recv()
            zs[last, j] += zr[n_layer, j]

    def loop(count, body):
        lax.fori_loop(0, count, lambda i, carry: (body(i), carry)[1], 0)

    def mask_x(j):
        tile = (j * wc) // TILE
        for t in range(row_tiles):
            keep = pp[t * width_tiles + tile].astype(F32)
            xg[0, r, j, t * TILE:(t + 1) * TILE, :] = (
                x_ref[t * TILE:(t + 1) * TILE, pl.ds(pl.multiple_of(j * wc, wc), wc)] * keep
            )

    def mask_a(s, h):
        load_a(s, h).wait()
        a = order(s)
        part = pl.ds(pl.multiple_of(h * rc, rc), rc)
        for t in range(depth_tiles):
            keep = mp[(h * rc) // TILE * depth_tiles + t, a].astype(F32)
            a_send[a, part, t * TILE:(t + 1) * TILE] = a_ref[a, part, t * TILE:(t + 1) * TILE] * keep

    loop(n_layer * ROW_CHUNKS, lambda u: load_a(u // ROW_CHUNKS, u % ROW_CHUNKS).start())
    loop(COLUMN_CHUNKS, mask_x)
    mask_a(0, 0)
    pl.semaphore_wait(barrier, n_col - 1 + n_row * n_layer - 1)

    def send_a(s, h):
        for o in range(1, n_col):
            a_copy(o, s, h).start()

    def send_x(step, h):
        for j in range(COLUMN_CHUNKS):
            for copy in x_copies(step, j, h):
                copy.start()

    send_a(0, 0)
    loop(ROW_CHUNKS, lambda h: send_x(0, h))

    def start_a(u):
        s, h = u // ROW_CHUNKS, u % ROW_CHUNKS

        @pl.when(u > 0)
        def _():
            mask_a(s, h)
            send_a(s, h)

    loop(n_layer * ROW_CHUNKS, start_a)

    def own_a(u):
        s, h = u // ROW_CHUNKS, u % ROW_CHUNKS
        a = order(s)
        part = pl.ds(pl.multiple_of(h * rc, rc), rc)
        keep_a(c, a, part, a_send[a, part, :])

    loop(n_layer * ROW_CHUNKS, own_a)
    loop(COLUMN_CHUNKS, lambda j: forward(0, j))
    loop(COLUMN_CHUNKS, lambda j: finish(0, j))

    def first(s, h):
        a = order(s)
        part = pl.ds(pl.multiple_of(h * rc, rc), rc)
        for o in range(1, n_col):
            a_copy(o, s, h).wait_recv()
            keep_a(lax.rem(c + n_col - o, n_col), a, part, a_recv[o - 1, a, part, :])
        zs1[s, h] = product(a, part, pl.ds(0, width))
        return a, part

    def first_others(u):
        s, h = u // ROW_CHUNKS, u % ROW_CHUNKS
        a, part = first(s, h)
        pass_on(zs1, zr1, z1_ss, z1_rs, a, s, h)

    loop((n_layer - 1) * ROW_CHUNKS, first_others)

    def first_own(h):
        a, part = first(n_layer - 1, h)
        receive_own(zs1, zr1, z1_ss, z1_rs, h)
        for j in range(COLUMN_CHUNKS):
            xg[1, r, j, part, :] = zs1[n_layer - 1, h, :, j * wc:(j + 1) * wc]
        send_x(1, h)

    loop(ROW_CHUNKS, first_own)

    whole = pl.ds(0, rows)

    def others(j):
        columns = pl.ds(pl.multiple_of(j * wc, wc), wc)
        finish(1, j)

        def each(s):
            a = order(s)
            zs2[s, j] = product(a, whole, columns)
            pass_on(zs2, zr2, z2_ss, z2_rs, a, s, j)

        loop(n_layer - 1, each)

    def own(j):
        columns = pl.ds(pl.multiple_of(j * wc, wc), wc)
        zs2[n_layer - 1, j] = product(l, whole, columns)
        receive_own(zs2, zr2, z2_ss, z2_rs, j)
        tile = (j * wc) // TILE
        total = jnp.zeros((1, wc), F32)
        kept = jnp.zeros((1, wc), F32)
        for t in range(row_tiles):
            keep = op[t * width_tiles + tile].astype(F32)
            value = zs2[n_layer - 1, j, t * TILE:(t + 1) * TILE, :]
            squared = value * value * keep
            sq_ref[t * TILE:(t + 1) * TILE, columns] = squared
            total += jnp.sum(squared, axis=0, keepdims=True)
            kept += keep * TILE
        tots[me, 0:1, columns] = total
        tots[me, 1:2, columns] = kept

    peers = n_row * n_layer
    me = r * n_layer + l

    def t_copy(o):
        to_row, to_layer = lax.rem(r + o // n_layer, n_row), lax.rem(l + o % n_layer, n_layer)
        return remote(tots.at[me], tots.at[me], t_ss.at[o - 1], t_rs.at[o - 1], row=to_row, layer=to_layer)

    forward(1, 0)

    def second(j):
        @pl.when(j < COLUMN_CHUNKS)
        def _():
            others(j)

        @pl.when(j < COLUMN_CHUNKS - 1)
        def _():
            forward(1, j + 1)

        @pl.when(j > 0)
        def _():
            own(j - 1)

    loop(COLUMN_CHUNKS + 1, second)

    for o in range(1, peers):
        t_copy(o).start()
    for o in range(1, peers):
        source_row, source_layer = lax.rem(r + n_row - o // n_layer, n_row), lax.rem(l + n_layer - o % n_layer, n_layer)
        landed = tots.at[source_row * n_layer + source_layer]
        remote(landed, landed, t_ss.at[o - 1], t_rs.at[o - 1], row=source_row, layer=source_layer).wait_recv()
    everywhere = tots[0]
    for i in range(1, peers):
        everywhere += tots[i]
    fac_ref[...] = everywhere[1:2] / everywhere[0:1]

    def a_left(u):
        s, h = u // ROW_CHUNKS, u % ROW_CHUNKS
        for o in range(1, n_col):
            a_copy(o, s, h).wait_send()

    loop(n_layer * ROW_CHUNKS, a_left)

    def z1_left(u):
        s, h = u // ROW_CHUNKS, u % ROW_CHUNKS
        block = zs1.at[s, h]
        remote(block, block, z1_ss.at[s, h], z1_rs.at[0, h], layer=lax.rem(l + 1, n_layer)).wait_send()

    loop((n_layer - 1) * ROW_CHUNKS, z1_left)

    def chunk_left(j):
        for step in range(2):
            for h in range(ROW_CHUNKS):
                for copy in x_copies(step, j, h):
                    copy.wait_send()
                for o in range(1, n_x):
                    x_forward(step, j, h, o).wait_send()
        for s in range(n_layer - 1):
            block = zs2.at[s, j]
            remote(block, block, z2_ss.at[s, j], z2_rs.at[0, j], layer=lax.rem(l + 1, n_layer)).wait_send()

    loop(COLUMN_CHUNKS, chunk_left)
    for o in range(1, peers):
        t_copy(o).wait_send()


def body(sizes, matrix_values, matrix_pattern, panel, panel_pattern, out_pattern):
    n_row, n_col, n_layer = sizes
    slabs, rows, _, depth = matrix_values.shape
    width = panel.shape[2]
    inner = depth * n_col
    rc, wc = rows // ROW_CHUNKS, width // COLUMN_CHUNKS
    n_x = n_row // 2
    dma = pltpu.SemaphoreType.DMA
    squared, factor = pl.pallas_call(
        functools.partial(kernel, sizes),
        out_shape=(
            jax.ShapeDtypeStruct((rows, width), F32),
            jax.ShapeDtypeStruct((1, width), F32),
        ),
        in_specs=[pl.BlockSpec(memory_space=pltpu.SMEM)] * 3
        + [pl.BlockSpec(memory_space=pl.ANY), pl.BlockSpec(memory_space=pltpu.VMEM)],
        out_specs=(pl.BlockSpec(memory_space=pltpu.VMEM),) * 2,
        scratch_shapes=[
            pltpu.VMEM((slabs, rows, depth), F32),
            pltpu.VMEM((slabs, rows, depth), F32),
            pltpu.VMEM((n_col - 1, slabs, rows, depth), F32),
            pltpu.VMEM((slabs, rows, inner), BF16),
            pltpu.VMEM((slabs, rows, inner), BF16),
            pltpu.VMEM((2, n_row, COLUMN_CHUNKS, rows, wc), F32),
            pltpu.VMEM((inner, width), BF16),
            pltpu.VMEM((inner, width), BF16),
            pltpu.VMEM((n_layer, ROW_CHUNKS, rc, width), F32),
            pltpu.VMEM((n_layer + 1, ROW_CHUNKS, rc, width), F32),
            pltpu.VMEM((n_layer, COLUMN_CHUNKS, rows, wc), F32),
            pltpu.VMEM((n_layer + 1, COLUMN_CHUNKS, rows, wc), F32),
            pltpu.VMEM((n_row * n_layer, 2, width), F32),
            dma((n_layer, ROW_CHUNKS)),
            dma((n_col - 1, n_layer, ROW_CHUNKS)),
            dma((n_col - 1, n_layer, ROW_CHUNKS)),
            dma((2, COLUMN_CHUNKS, ROW_CHUNKS, n_x)),
            dma((2, COLUMN_CHUNKS, ROW_CHUNKS, n_x)),
            dma((2, COLUMN_CHUNKS, ROW_CHUNKS, n_row)),
            dma((n_layer, ROW_CHUNKS)),
            dma((n_layer + 1, ROW_CHUNKS)),
            dma((n_layer, COLUMN_CHUNKS)),
            dma((n_layer + 1, COLUMN_CHUNKS)),
            dma((n_row * n_layer - 1,)),
            dma((n_row * n_layer - 1,)),
        ],
        compiler_params=pltpu.CompilerParams(
            collective_id=0, has_side_effects=True, vmem_limit_bytes=56 * 1024 * 1024
        ),
        name="walk",
    )(
        jnp.transpose(matrix_pattern, (1, 2, 3, 0)).reshape(-1, slabs),
        panel_pattern.reshape(-1),
        out_pattern.reshape(-1),
        matrix_values,
        panel.reshape(rows, width),
    )
    return (squared * factor)[None]


def solution(mesh):
    placed = (
        P(None, "row", "layer", "col"),
        P(None, "row", "layer", "col"),
        P("layer", "row", "col"),
        P("layer", "row", "col"),
        P("layer", "row", "col"),
    )
    sizes = (mesh.shape["row"], mesh.shape["col"], mesh.shape["layer"])
    return jax.shard_map(
        functools.partial(body, sizes), mesh=mesh, in_specs=placed, out_specs=P("layer", "row", "col"),
        check_vma=False,
    )
```

```python
import functools

import jax
import jax.numpy as jnp
from jax import lax
from jax.experimental import pallas as pl
from jax.experimental.pallas import tpu as pltpu
from jax.sharding import PartitionSpec as P

TILE = 256
MESH = pl.DeviceIdType.MESH
ROW_CHUNKS = 2
COLUMN_CHUNKS = 4
F32 = jnp.float32
BF16 = jnp.bfloat16


def slab_order(layers):
    table = []
    for layer in range(layers):
        up = list(range(layers - 1, layer, -1))
        down = list(range(layer))
        first, second = (up, down) if len(up) >= len(down) else (down, up)
        order = []
        for i in range(len(first)):
            order.append(first[i])
            if i < len(second):
                order.append(second[i])
        table.append(order + [layer])
    return table


def split(value):
    high = value.astype(BF16)
    return high, (value - high.astype(F32)).astype(BF16)


def kernel(
    sizes, mp, pp, op, a_hbm, x_hbm, sq_hbm, fac_ref,
    a_ref, x_ref, sq_ref, a_send, a_recv, ah, al, xg, xh, xl, zs1, zr1, zs2, zr2, tots,
    x_ls, sq_ss, a_ls, a_ss, a_rs, x_ss, x_fs, x_rs, z1_ss, z1_rs, z2_ss, z2_rs, t_ss, t_rs,
):
    n_row, n_col, n_layer = sizes
    slabs, rows, depth = a_ref.shape
    width = x_ref.shape[1]
    rc = rows // ROW_CHUNKS
    wc = width // COLUMN_CHUNKS
    row_tiles, depth_tiles, width_tiles = rows // TILE, depth // TILE, width // TILE
    r, c, l = lax.axis_index("row"), lax.axis_index("col"), lax.axis_index("layer")
    sibling = r + 1 - 2 * lax.rem(r, 2)
    n_x = n_row // 2
    table = slab_order(n_layer)

    def order(s):
        index = l * n_layer + s
        a = jnp.int32(0)
        for i in range(n_layer):
            for j in range(n_layer):
                if table[i][j]:
                    a = jnp.where(index == i * n_layer + j, table[i][j], a)
        return a

    def remote(src, dst, ss, rs, **device):
        return pltpu.make_async_remote_copy(
            src_ref=src, dst_ref=dst, send_sem=ss, recv_sem=rs, device_id=device, device_id_type=MESH
        )

    barrier = pltpu.get_barrier_semaphore()
    for o in range(1, n_col):
        pl.semaphore_signal(barrier, inc=1, device_id={"col": lax.rem(c + o, n_col)}, device_id_type=MESH)
    peers = n_row * n_layer
    me = r * n_layer + l
    for o in range(1, peers):
        to_row, to_layer = lax.rem(r + o // n_layer, n_row), lax.rem(l + o % n_layer, n_layer)
        pl.semaphore_signal(barrier, inc=1, device_id={"row": to_row, "layer": to_layer}, device_id_type=MESH)

    def t_copy(kind, o):
        to_row, to_layer = lax.rem(r + o // n_layer, n_row), lax.rem(l + o % n_layer, n_layer)
        own_row = tots.at[kind, me]
        return remote(own_row, own_row, t_ss.at[kind, o - 1], t_rs.at[kind, o - 1], row=to_row, layer=to_layer)

    def t_landed(kind, o):
        source_row, source_layer = lax.rem(r + n_row - o // n_layer, n_row), lax.rem(l + n_layer - o % n_layer, n_layer)
        landed = tots.at[kind, source_row * n_layer + source_layer]
        return remote(landed, landed, t_ss.at[kind, o - 1], t_rs.at[kind, o - 1], row=source_row, layer=source_layer)

    def load_a(s, h):
        a = order(s)
        part = pl.ds(pl.multiple_of(h * rc, rc), rc)
        return pltpu.make_async_copy(a_hbm.at[a, part, 0, :], a_ref.at[a, part, :], a_ls.at[s, h])

    def x_block(step, source, j, h):
        return xg.at[step, source, j, pl.ds(pl.multiple_of(h * rc, rc), rc), :]

    def x_copies(step, j, h):
        own = x_block(step, r, j, h)
        yield remote(own, own, x_ss.at[step, j, h, 0], x_rs.at[step, j, h, r], row=sibling)
        for o in range(1, n_x):
            yield remote(own, own, x_ss.at[step, j, h, o], x_rs.at[step, j, h, r], row=lax.rem(r + 2 * o, n_row))

    def x_forward(step, j, h, o):
        source = lax.rem(r + n_row - 2 * o, n_row)
        block = x_block(step, source, j, h)
        return remote(block, block, x_fs.at[step, j, h, o - 1], x_rs.at[step, j, h, source], row=sibling)

    def forward(step, j):
        for h in range(ROW_CHUNKS):
            for o in range(1, n_x):
                copy = x_forward(step, j, h, o)
                copy.wait_recv()
                copy.start()

    def finish(step, j):
        for h in range(ROW_CHUNKS):
            for o in range(n_x):
                source = lax.rem(sibling + n_row - 2 * o, n_row)
                block = x_block(step, source, j, h)
                remote(block, block, x_ss.at[step, j, h, 0], x_rs.at[step, j, h, source], row=sibling).wait_recv()
        columns = pl.ds(pl.multiple_of(j * wc, wc), wc)
        for source in range(n_row):
            high, low = split(xg[step, source, j])
            xh[source * rows:(source + 1) * rows, columns] = high
            xl[source * rows:(source + 1) * rows, columns] = low

    def a_copy(o, s, h):
        a = order(s)
        part = pl.ds(pl.multiple_of(h * rc, rc), rc)
        return remote(
            a_send.at[a, part, :], a_recv.at[o - 1, a, part, :], a_ss.at[o - 1, s, h], a_rs.at[o - 1, s, h],
            col=lax.rem(c + o, n_col),
        )

    def keep_a(source, a, part, value):
        columns = pl.ds(pl.multiple_of(source * depth, depth), depth)
        high, low = split(value)
        ah[a, part, columns] = high
        al[a, part, columns] = low

    def product(a, part, columns):
        high = ah[a, part, :]
        right = xh[:, columns]
        total = jnp.dot(high, right, preferred_element_type=F32)
        total += jnp.dot(high, xl[:, columns], preferred_element_type=F32)
        return total + jnp.dot(al[a, part, :], right, preferred_element_type=F32)

    def pass_on(zs, zr, ss, rs, a, s, j):
        upward = a > l
        slot = jnp.where(a == l - 1, n_layer, a)
        target = jnp.where(upward, l + 1, l - 1)

        @pl.when(jnp.where(upward, l, n_layer - 1 - l) > 0)
        def _():
            remote(zs.at[s, j], zr.at[a, j], ss.at[s, j], rs.at[a, j], layer=target).wait_recv()
            zs[s, j] += zr[a, j]

        remote(zs.at[s, j], zr.at[slot, j], ss.at[s, j], rs.at[slot, j], layer=target).start()

    def receive_own(zs, zr, ss, rs, j):
        last = n_layer - 1

        @pl.when(l > 0)
        def _():
            remote(zs.at[last, j], zr.at[l, j], ss.at[0, j], rs.at[l, j], layer=l - 1).wait_recv()
            zs[last, j] += zr[l, j]

        @pl.when(l < last)
        def _():
            remote(zs.at[last, j], zr.at[n_layer, j], ss.at[0, j], rs.at[n_layer, j], layer=l + 1).wait_recv()
            zs[last, j] += zr[n_layer, j]

    def loop(count, body):
        lax.fori_loop(0, count, lambda i, carry: (body(i), carry)[1], 0)

    def mask_x(j):
        tile = (j * wc) // TILE
        for t in range(row_tiles):
            keep = pp[t * width_tiles + tile].astype(F32)
            xg[0, r, j, t * TILE:(t + 1) * TILE, :] = (
                x_ref[t * TILE:(t + 1) * TILE, pl.ds(pl.multiple_of(j * wc, wc), wc)] * keep
            )

    def mask_a(s, h):
        load_a(s, h).wait()
        a = order(s)
        part = pl.ds(pl.multiple_of(h * rc, rc), rc)
        for t in range(depth_tiles):
            keep = mp[(h * rc) // TILE * depth_tiles + t, a].astype(F32)
            a_send[a, part, t * TILE:(t + 1) * TILE] = a_ref[a, part, t * TILE:(t + 1) * TILE] * keep

    loop(n_layer * ROW_CHUNKS, lambda u: load_a(u // ROW_CHUNKS, u % ROW_CHUNKS).start())
    x_load = pltpu.make_async_copy(x_hbm, x_ref, x_ls)
    x_load.start()
    mask_a(0, 0)
    pl.semaphore_wait(barrier, n_col - 1 + n_row * n_layer - 1)

    def send_a(s, h):
        for o in range(1, n_col):
            a_copy(o, s, h).start()

    def send_x(step, h):
        for j in range(COLUMN_CHUNKS):
            for copy in x_copies(step, j, h):
                copy.start()

    send_a(0, 0)
    x_load.wait()
    loop(COLUMN_CHUNKS, mask_x)
    loop(ROW_CHUNKS, lambda h: send_x(0, h))

    def start_a(u):
        s, h = u // ROW_CHUNKS, u % ROW_CHUNKS

        @pl.when(u > 0)
        def _():
            mask_a(s, h)
            send_a(s, h)

    loop(n_layer * ROW_CHUNKS, start_a)

    def own_a(u):
        s, h = u // ROW_CHUNKS, u % ROW_CHUNKS
        a = order(s)
        part = pl.ds(pl.multiple_of(h * rc, rc), rc)
        keep_a(c, a, part, a_send[a, part, :])

    loop(n_layer * ROW_CHUNKS, own_a)
    for tile in range(width_tiles):
        kept = jnp.zeros((1, TILE), F32)
        for t in range(row_tiles):
            kept += op[t * width_tiles + tile].astype(F32) * TILE
        tots[0, me, :, tile * TILE:(tile + 1) * TILE] = kept
    for o in range(1, peers):
        t_copy(0, o).start()
    loop(COLUMN_CHUNKS, lambda j: forward(0, j))
    loop(COLUMN_CHUNKS, lambda j: finish(0, j))

    def first(s, h):
        a = order(s)
        part = pl.ds(pl.multiple_of(h * rc, rc), rc)
        for o in range(1, n_col):
            a_copy(o, s, h).wait_recv()
            keep_a(lax.rem(c + n_col - o, n_col), a, part, a_recv[o - 1, a, part, :])
        zs1[s, h] = product(a, part, pl.ds(0, width))
        return a, part

    def first_others(u):
        s, h = u // ROW_CHUNKS, u % ROW_CHUNKS
        a, part = first(s, h)
        pass_on(zs1, zr1, z1_ss, z1_rs, a, s, h)

    loop((n_layer - 1) * ROW_CHUNKS, first_others)

    def first_own(h):
        a, part = first(n_layer - 1, h)
        receive_own(zs1, zr1, z1_ss, z1_rs, h)
        for j in range(COLUMN_CHUNKS):
            xg[1, r, j, part, :] = zs1[n_layer - 1, h, :, j * wc:(j + 1) * wc]
        send_x(1, h)

    loop(ROW_CHUNKS, first_own)

    whole = pl.ds(0, rows)

    def others(j):
        columns = pl.ds(pl.multiple_of(j * wc, wc), wc)
        finish(1, j)

        def each(s):
            a = order(s)
            zs2[s, j] = product(a, whole, columns)
            pass_on(zs2, zr2, z2_ss, z2_rs, a, s, j)

        loop(n_layer - 1, each)

    def sq_copy(j):
        columns = pl.ds(pl.multiple_of(j * wc, wc), wc)
        return pltpu.make_async_copy(sq_ref.at[:, columns], sq_hbm.at[:, columns], sq_ss.at[j])

    def own(j):
        columns = pl.ds(pl.multiple_of(j * wc, wc), wc)
        zs2[n_layer - 1, j] = product(l, whole, columns)
        receive_own(zs2, zr2, z2_ss, z2_rs, j)
        tile = (j * wc) // TILE
        total = jnp.zeros((1, wc), F32)
        for t in range(row_tiles):
            keep = op[t * width_tiles + tile].astype(F32)
            value = zs2[n_layer - 1, j, t * TILE:(t + 1) * TILE, :]
            squared = value * value * keep
            sq_ref[t * TILE:(t + 1) * TILE, columns] = squared
            total += jnp.sum(squared, axis=0, keepdims=True)
        tots[1, me, :, columns] = total
        sq_copy(j).start()

    forward(1, 0)

    def second(j):
        @pl.when(j < COLUMN_CHUNKS)
        def _():
            others(j)

        @pl.when(j < COLUMN_CHUNKS - 1)
        def _():
            forward(1, j + 1)

        @pl.when(j > 0)
        def _():
            own(j - 1)

    loop(COLUMN_CHUNKS + 1, second)

    for o in range(1, peers):
        t_copy(1, o).start()
    for o in range(1, peers):
        t_landed(0, o).wait_recv()
    counted = sum(tots[0, i] for i in range(peers))
    for o in range(1, peers):
        t_landed(1, o).wait_recv()
    fac_ref[...] = counted / sum(tots[1, i] for i in range(peers))

    def a_left(u):
        s, h = u // ROW_CHUNKS, u % ROW_CHUNKS
        for o in range(1, n_col):
            a_copy(o, s, h).wait_send()

    loop(n_layer * ROW_CHUNKS, a_left)

    def z1_left(u):
        s, h = u // ROW_CHUNKS, u % ROW_CHUNKS
        block = zs1.at[s, h]
        remote(block, block, z1_ss.at[s, h], z1_rs.at[0, h], layer=lax.rem(l + 1, n_layer)).wait_send()

    loop((n_layer - 1) * ROW_CHUNKS, z1_left)

    def chunk_left(j):
        for step in range(2):
            for h in range(ROW_CHUNKS):
                for copy in x_copies(step, j, h):
                    copy.wait_send()
                for o in range(1, n_x):
                    x_forward(step, j, h, o).wait_send()
        for s in range(n_layer - 1):
            block = zs2.at[s, j]
            remote(block, block, z2_ss.at[s, j], z2_rs.at[0, j], layer=lax.rem(l + 1, n_layer)).wait_send()

    loop(COLUMN_CHUNKS, chunk_left)
    loop(COLUMN_CHUNKS, lambda j: sq_copy(j).wait())
    for o in range(1, peers):
        t_copy(0, o).wait_send()
        t_copy(1, o).wait_send()


def body(sizes, matrix_values, matrix_pattern, panel, panel_pattern, out_pattern):
    n_row, n_col, n_layer = sizes
    slabs, rows, _, depth = matrix_values.shape
    width = panel.shape[2]
    inner = depth * n_col
    rc, wc = rows // ROW_CHUNKS, width // COLUMN_CHUNKS
    n_x = n_row // 2
    dma = pltpu.SemaphoreType.DMA
    squared, factor = pl.pallas_call(
        functools.partial(kernel, sizes),
        out_shape=(
            jax.ShapeDtypeStruct((rows, width), F32),
            jax.ShapeDtypeStruct((1, width), F32),
        ),
        in_specs=[pl.BlockSpec(memory_space=pltpu.SMEM)] * 3
        + [pl.BlockSpec(memory_space=pl.ANY)] * 2,
        out_specs=(pl.BlockSpec(memory_space=pl.ANY), pl.BlockSpec(memory_space=pltpu.VMEM)),
        scratch_shapes=[
            pltpu.VMEM((slabs, rows, depth), F32),
            pltpu.VMEM((rows, width), F32),
            pltpu.VMEM((rows, width), F32),
            pltpu.VMEM((slabs, rows, depth), F32),
            pltpu.VMEM((n_col - 1, slabs, rows, depth), F32),
            pltpu.VMEM((slabs, rows, inner), BF16),
            pltpu.VMEM((slabs, rows, inner), BF16),
            pltpu.VMEM((2, n_row, COLUMN_CHUNKS, rows, wc), F32),
            pltpu.VMEM((inner, width), BF16),
            pltpu.VMEM((inner, width), BF16),
            pltpu.VMEM((n_layer, ROW_CHUNKS, rc, width), F32),
            pltpu.VMEM((n_layer + 1, ROW_CHUNKS, rc, width), F32),
            pltpu.VMEM((n_layer, COLUMN_CHUNKS, rows, wc), F32),
            pltpu.VMEM((n_layer + 1, COLUMN_CHUNKS, rows, wc), F32),
            pltpu.VMEM((2, n_row * n_layer, 1, width), F32),
            dma,
            dma((COLUMN_CHUNKS,)),
            dma((n_layer, ROW_CHUNKS)),
            dma((n_col - 1, n_layer, ROW_CHUNKS)),
            dma((n_col - 1, n_layer, ROW_CHUNKS)),
            dma((2, COLUMN_CHUNKS, ROW_CHUNKS, n_x)),
            dma((2, COLUMN_CHUNKS, ROW_CHUNKS, n_x)),
            dma((2, COLUMN_CHUNKS, ROW_CHUNKS, n_row)),
            dma((n_layer, ROW_CHUNKS)),
            dma((n_layer + 1, ROW_CHUNKS)),
            dma((n_layer, COLUMN_CHUNKS)),
            dma((n_layer + 1, COLUMN_CHUNKS)),
            dma((2, n_row * n_layer - 1)),
            dma((2, n_row * n_layer - 1)),
        ],
        compiler_params=pltpu.CompilerParams(
            collective_id=0, has_side_effects=True, vmem_limit_bytes=56 * 1024 * 1024
        ),
        name="walk",
    )(
        jnp.transpose(matrix_pattern, (1, 2, 3, 0)).reshape(-1, slabs),
        panel_pattern.reshape(-1),
        out_pattern.reshape(-1),
        matrix_values,
        panel.reshape(rows, width),
    )
    return (squared * factor)[None]


def solution(mesh):
    placed = (
        P(None, "row", "layer", "col"),
        P(None, "row", "layer", "col"),
        P("layer", "row", "col"),
        P("layer", "row", "col"),
        P("layer", "row", "col"),
    )
    sizes = (mesh.shape["row"], mesh.shape["col"], mesh.shape["layer"])
    return jax.shard_map(
        functools.partial(body, sizes), mesh=mesh, in_specs=placed, out_specs=P("layer", "row", "col"),
        check_vma=False,
    )
```

```python
import functools

import jax
import jax.numpy as jnp
from jax import lax
from jax.experimental import pallas as pl
from jax.experimental.pallas import tpu as pltpu
from jax.sharding import PartitionSpec as P

TILE = 256
MESH = pl.DeviceIdType.MESH
ROW_CHUNKS = 2
COLUMN_CHUNKS = 4
F32 = jnp.float32
BF16 = jnp.bfloat16


def slab_order(layers):
    table = []
    for layer in range(layers):
        up = list(range(layers - 1, layer, -1))
        down = list(range(layer))
        first, second = (up, down) if len(up) >= len(down) else (down, up)
        order = []
        for i in range(len(first)):
            order.append(first[i])
            if i < len(second):
                order.append(second[i])
        table.append(order + [layer])
    return table


def split(value):
    high = value.astype(BF16)
    return high, (value - high.astype(F32)).astype(BF16)


def kernel(
    sizes, mp, pp, op, a_hbm, x_hbm, sq_hbm, fac_ref,
    a_ref, x_ref, sq_ref, a_send, a_recv, ah, al, xg, xh, xl, zs1, zr1, zs2, zr2, tots,
    x_ls, sq_ss, a_ls, a_ss, a_rs, x_ss, x_fs, x_rs, z1_ss, z1_rs, z2_ss, z2_rs, t_ss, t_rs,
):
    n_row, n_col, n_layer = sizes
    slabs, rows, depth = a_ref.shape
    width = x_ref.shape[1]
    rc = rows // ROW_CHUNKS
    wc = width // COLUMN_CHUNKS
    row_tiles, depth_tiles, width_tiles = rows // TILE, depth // TILE, width // TILE
    r, c, l = lax.axis_index("row"), lax.axis_index("col"), lax.axis_index("layer")
    sibling = r + 1 - 2 * lax.rem(r, 2)
    n_x = n_row // 2
    table = slab_order(n_layer)

    def order(s):
        index = l * n_layer + s
        a = jnp.int32(0)
        for i in range(n_layer):
            for j in range(n_layer):
                if table[i][j]:
                    a = jnp.where(index == i * n_layer + j, table[i][j], a)
        return a

    def remote(src, dst, ss, rs, **device):
        return pltpu.make_async_remote_copy(
            src_ref=src, dst_ref=dst, send_sem=ss, recv_sem=rs, device_id=device, device_id_type=MESH
        )

    barrier = pltpu.get_barrier_semaphore()
    for o in range(1, n_col):
        pl.semaphore_signal(barrier, inc=1, device_id={"col": lax.rem(c + o, n_col)}, device_id_type=MESH)
    peers = n_row * n_layer
    me = r * n_layer + l
    for o in range(1, peers):
        to_row, to_layer = lax.rem(r + o // n_layer, n_row), lax.rem(l + o % n_layer, n_layer)
        pl.semaphore_signal(barrier, inc=1, device_id={"row": to_row, "layer": to_layer}, device_id_type=MESH)

    def t_copy(kind, o):
        to_row, to_layer = lax.rem(r + o // n_layer, n_row), lax.rem(l + o % n_layer, n_layer)
        own_row = tots.at[kind, me]
        return remote(own_row, own_row, t_ss.at[kind, o - 1], t_rs.at[kind, o - 1], row=to_row, layer=to_layer)

    def t_landed(kind, o):
        source_row, source_layer = lax.rem(r + n_row - o // n_layer, n_row), lax.rem(l + n_layer - o % n_layer, n_layer)
        landed = tots.at[kind, source_row * n_layer + source_layer]
        return remote(landed, landed, t_ss.at[kind, o - 1], t_rs.at[kind, o - 1], row=source_row, layer=source_layer)

    def load_a(s, h):
        a = order(s)
        part = pl.ds(pl.multiple_of(h * rc, rc), rc)
        return pltpu.make_async_copy(a_hbm.at[a, part, 0, :], a_ref.at[a, part, :], a_ls.at[s, h])

    def x_block(step, source, j, h):
        return xg.at[step, source, j, pl.ds(pl.multiple_of(h * rc, rc), rc), :]

    def x_copies(step, j, h):
        own = x_block(step, r, j, h)
        yield remote(own, own, x_ss.at[step, j, h, 0], x_rs.at[step, j, h, r], row=sibling)
        for o in range(1, n_x):
            yield remote(own, own, x_ss.at[step, j, h, o], x_rs.at[step, j, h, r], row=lax.rem(r + 2 * o, n_row))

    def x_forward(step, j, h, o):
        source = lax.rem(r + n_row - 2 * o, n_row)
        block = x_block(step, source, j, h)
        return remote(block, block, x_fs.at[step, j, h, o - 1], x_rs.at[step, j, h, source], row=sibling)

    def forward(step, j):
        for h in range(ROW_CHUNKS):
            for o in range(1, n_x):
                copy = x_forward(step, j, h, o)
                copy.wait_recv()
                copy.start()

    def finish(step, j):
        for h in range(ROW_CHUNKS):
            for o in range(n_x):
                source = lax.rem(sibling + n_row - 2 * o, n_row)
                block = x_block(step, source, j, h)
                remote(block, block, x_ss.at[step, j, h, 0], x_rs.at[step, j, h, source], row=sibling).wait_recv()
        columns = pl.ds(pl.multiple_of(j * wc, wc), wc)
        for source in range(n_row):
            high, low = split(xg[step, source, j])
            xh[source * rows:(source + 1) * rows, columns] = high
            xl[source * rows:(source + 1) * rows, columns] = low

    def a_copy(o, s, h):
        a = order(s)
        part = pl.ds(pl.multiple_of(h * rc, rc), rc)
        return remote(
            a_send.at[a, part, :], a_recv.at[o - 1, a, part, :], a_ss.at[o - 1, s, h], a_rs.at[o - 1, s, h],
            col=lax.rem(c + o, n_col),
        )

    def keep_a(source, a, part, value):
        columns = pl.ds(pl.multiple_of(source * depth, depth), depth)
        high, low = split(value)
        ah[a, part, columns] = high
        al[a, part, columns] = low

    def product(a, part, columns):
        high = ah[a, part, :]
        right = xh[:, columns]
        total = jnp.dot(high, right, preferred_element_type=F32)
        total += jnp.dot(high, xl[:, columns], preferred_element_type=F32)
        return total + jnp.dot(al[a, part, :], right, preferred_element_type=F32)

    def pass_on(zs, zr, ss, rs, a, s, j):
        upward = a > l
        slot = jnp.where(a == l - 1, n_layer, a)
        target = jnp.where(upward, l + 1, l - 1)

        @pl.when(jnp.where(upward, l, n_layer - 1 - l) > 0)
        def _():
            remote(zs.at[s, j], zr.at[a, j], ss.at[s, j], rs.at[a, j], layer=target).wait_recv()
            zs[s, j] += zr[a, j]

        remote(zs.at[s, j], zr.at[slot, j], ss.at[s, j], rs.at[slot, j], layer=target).start()

    def receive_own(zs, zr, ss, rs, j):
        last = n_layer - 1

        @pl.when(l > 0)
        def _():
            remote(zs.at[last, j], zr.at[l, j], ss.at[0, j], rs.at[l, j], layer=l - 1).wait_recv()
            zs[last, j] += zr[l, j]

        @pl.when(l < last)
        def _():
            remote(zs.at[last, j], zr.at[n_layer, j], ss.at[0, j], rs.at[n_layer, j], layer=l + 1).wait_recv()
            zs[last, j] += zr[n_layer, j]

    def loop(count, body):
        lax.fori_loop(0, count, lambda i, carry: (body(i), carry)[1], 0)

    def mask_x(j):
        tile = (j * wc) // TILE
        for t in range(row_tiles):
            keep = pp[t * width_tiles + tile].astype(F32)
            xg[0, r, j, t * TILE:(t + 1) * TILE, :] = (
                x_ref[t * TILE:(t + 1) * TILE, pl.ds(pl.multiple_of(j * wc, wc), wc)] * keep
            )

    def mask_a(s, h):
        load_a(s, h).wait()
        a = order(s)
        part = pl.ds(pl.multiple_of(h * rc, rc), rc)
        for t in range(depth_tiles):
            keep = mp[(h * rc) // TILE * depth_tiles + t, a].astype(F32)
            a_send[a, part, t * TILE:(t + 1) * TILE] = a_ref[a, part, t * TILE:(t + 1) * TILE] * keep

    loop(n_layer * ROW_CHUNKS, lambda u: load_a(u // ROW_CHUNKS, u % ROW_CHUNKS).start())
    x_load = pltpu.make_async_copy(x_hbm, x_ref, x_ls)
    x_load.start()
    mask_a(0, 0)
    pl.semaphore_wait(barrier, n_col - 1 + n_row * n_layer - 1)

    def send_a(s, h):
        for o in range(1, n_col):
            a_copy(o, s, h).start()

    def send_x(step, h):
        for j in range(COLUMN_CHUNKS):
            for copy in x_copies(step, j, h):
                copy.start()

    send_a(0, 0)
    x_load.wait()
    loop(COLUMN_CHUNKS, mask_x)
    loop(ROW_CHUNKS, lambda h: send_x(0, h))

    def start_a(u):
        s, h = u // ROW_CHUNKS, u % ROW_CHUNKS

        @pl.when(u > 0)
        def _():
            mask_a(s, h)
            send_a(s, h)

    loop(n_layer * ROW_CHUNKS, start_a)

    def own_a(u):
        s, h = u // ROW_CHUNKS, u % ROW_CHUNKS
        a = order(s)
        part = pl.ds(pl.multiple_of(h * rc, rc), rc)
        keep_a(c, a, part, a_send[a, part, :])

    loop(n_layer * ROW_CHUNKS, own_a)
    for tile in range(width_tiles):
        kept = jnp.zeros((1, TILE), F32)
        for t in range(row_tiles):
            kept += op[t * width_tiles + tile].astype(F32) * TILE
        tots[0, me, :, tile * TILE:(tile + 1) * TILE] = kept
    for o in range(1, peers):
        t_copy(0, o).start()
    loop(COLUMN_CHUNKS, lambda j: forward(0, j))
    loop(COLUMN_CHUNKS, lambda j: finish(0, j))

    def first(s, h):
        a = order(s)
        part = pl.ds(pl.multiple_of(h * rc, rc), rc)
        for o in range(1, n_col):
            a_copy(o, s, h).wait_recv()
            keep_a(lax.rem(c + n_col - o, n_col), a, part, a_recv[o - 1, a, part, :])
        zs1[s, h] = product(a, part, pl.ds(0, width))
        return a, part

    def first_others(u):
        s, h = u // ROW_CHUNKS, u % ROW_CHUNKS
        a, part = first(s, h)
        pass_on(zs1, zr1, z1_ss, z1_rs, a, s, h)

    loop((n_layer - 1) * ROW_CHUNKS, first_others)

    def first_own(h):
        a, part = first(n_layer - 1, h)
        receive_own(zs1, zr1, z1_ss, z1_rs, h)
        for j in range(COLUMN_CHUNKS):
            xg[1, r, j, part, :] = zs1[n_layer - 1, h, :, j * wc:(j + 1) * wc]
        send_x(1, h)

    loop(ROW_CHUNKS, first_own)

    whole = pl.ds(0, rows)

    def others(j):
        columns = pl.ds(pl.multiple_of(j * wc, wc), wc)
        finish(1, j)

        def each(s):
            a = order(s)
            zs2[s, j] = product(a, whole, columns)
            pass_on(zs2, zr2, z2_ss, z2_rs, a, s, j)

        loop(n_layer - 1, each)

    def sq_copy(j):
        columns = pl.ds(pl.multiple_of(j * wc, wc), wc)
        return pltpu.make_async_copy(sq_ref.at[:, columns], sq_hbm.at[:, columns], sq_ss.at[j])

    def own(j):
        columns = pl.ds(pl.multiple_of(j * wc, wc), wc)
        zs2[n_layer - 1, j] = product(l, whole, columns)
        receive_own(zs2, zr2, z2_ss, z2_rs, j)
        tile = (j * wc) // TILE
        total = jnp.zeros((1, wc), F32)
        for t in range(row_tiles):
            keep = op[t * width_tiles + tile].astype(F32)
            value = zs2[n_layer - 1, j, t * TILE:(t + 1) * TILE, :]
            squared = value * value * keep
            sq_ref[t * TILE:(t + 1) * TILE, columns] = squared
            total += jnp.sum(squared, axis=0, keepdims=True)
        tots[1, me, :, columns] = total
        sq_copy(j).start()

    forward(1, 0)

    def second(j):
        @pl.when(j < COLUMN_CHUNKS)
        def _():
            others(j)

        @pl.when(j < COLUMN_CHUNKS - 1)
        def _():
            forward(1, j + 1)

        @pl.when(j > 0)
        def _():
            own(j - 1)

    loop(COLUMN_CHUNKS + 1, second)

    for o in range(1, peers):
        t_copy(1, o).start()

    def a_left(u):
        s, h = u // ROW_CHUNKS, u % ROW_CHUNKS
        for o in range(1, n_col):
            a_copy(o, s, h).wait_send()

    loop(n_layer * ROW_CHUNKS, a_left)

    def z1_left(u):
        s, h = u // ROW_CHUNKS, u % ROW_CHUNKS
        block = zs1.at[s, h]
        remote(block, block, z1_ss.at[s, h], z1_rs.at[0, h], layer=lax.rem(l + 1, n_layer)).wait_send()

    loop((n_layer - 1) * ROW_CHUNKS, z1_left)

    def chunk_left(j):
        for step in range(2):
            for h in range(ROW_CHUNKS):
                for copy in x_copies(step, j, h):
                    copy.wait_send()
                for o in range(1, n_x):
                    x_forward(step, j, h, o).wait_send()
        for s in range(n_layer - 1):
            block = zs2.at[s, j]
            remote(block, block, z2_ss.at[s, j], z2_rs.at[0, j], layer=lax.rem(l + 1, n_layer)).wait_send()

    loop(COLUMN_CHUNKS, chunk_left)
    loop(COLUMN_CHUNKS, lambda j: sq_copy(j).wait())
    for o in range(1, peers):
        t_copy(0, o).wait_send()

    for o in range(1, peers):
        t_landed(0, o).wait_recv()
    counted = sum(tots[0, i] for i in range(peers))
    for o in range(1, peers):
        t_landed(1, o).wait_recv()
    fac_ref[...] = counted / sum(tots[1, i] for i in range(peers))
    for o in range(1, peers):
        t_copy(1, o).wait_send()


def body(sizes, matrix_values, matrix_pattern, panel, panel_pattern, out_pattern):
    n_row, n_col, n_layer = sizes
    slabs, rows, _, depth = matrix_values.shape
    width = panel.shape[2]
    inner = depth * n_col
    rc, wc = rows // ROW_CHUNKS, width // COLUMN_CHUNKS
    n_x = n_row // 2
    dma = pltpu.SemaphoreType.DMA
    squared, factor = pl.pallas_call(
        functools.partial(kernel, sizes),
        out_shape=(
            jax.ShapeDtypeStruct((rows, width), F32),
            jax.ShapeDtypeStruct((1, width), F32),
        ),
        in_specs=[pl.BlockSpec(memory_space=pltpu.SMEM)] * 3
        + [pl.BlockSpec(memory_space=pl.ANY)] * 2,
        out_specs=(pl.BlockSpec(memory_space=pl.ANY), pl.BlockSpec(memory_space=pltpu.VMEM)),
        scratch_shapes=[
            pltpu.VMEM((slabs, rows, depth), F32),
            pltpu.VMEM((rows, width), F32),
            pltpu.VMEM((rows, width), F32),
            pltpu.VMEM((slabs, rows, depth), F32),
            pltpu.VMEM((n_col - 1, slabs, rows, depth), F32),
            pltpu.VMEM((slabs, rows, inner), BF16),
            pltpu.VMEM((slabs, rows, inner), BF16),
            pltpu.VMEM((2, n_row, COLUMN_CHUNKS, rows, wc), F32),
            pltpu.VMEM((inner, width), BF16),
            pltpu.VMEM((inner, width), BF16),
            pltpu.VMEM((n_layer, ROW_CHUNKS, rc, width), F32),
            pltpu.VMEM((n_layer + 1, ROW_CHUNKS, rc, width), F32),
            pltpu.VMEM((n_layer, COLUMN_CHUNKS, rows, wc), F32),
            pltpu.VMEM((n_layer + 1, COLUMN_CHUNKS, rows, wc), F32),
            pltpu.VMEM((2, n_row * n_layer, 1, width), F32),
            dma,
            dma((COLUMN_CHUNKS,)),
            dma((n_layer, ROW_CHUNKS)),
            dma((n_col - 1, n_layer, ROW_CHUNKS)),
            dma((n_col - 1, n_layer, ROW_CHUNKS)),
            dma((2, COLUMN_CHUNKS, ROW_CHUNKS, n_x)),
            dma((2, COLUMN_CHUNKS, ROW_CHUNKS, n_x)),
            dma((2, COLUMN_CHUNKS, ROW_CHUNKS, n_row)),
            dma((n_layer, ROW_CHUNKS)),
            dma((n_layer + 1, ROW_CHUNKS)),
            dma((n_layer, COLUMN_CHUNKS)),
            dma((n_layer + 1, COLUMN_CHUNKS)),
            dma((2, n_row * n_layer - 1)),
            dma((2, n_row * n_layer - 1)),
        ],
        compiler_params=pltpu.CompilerParams(
            collective_id=0, has_side_effects=True, vmem_limit_bytes=56 * 1024 * 1024
        ),
        name="walk",
    )(
        jnp.transpose(matrix_pattern, (1, 2, 3, 0)).reshape(-1, slabs),
        panel_pattern.reshape(-1),
        out_pattern.reshape(-1),
        matrix_values,
        panel.reshape(rows, width),
    )
    return (squared * factor)[None]


def solution(mesh):
    placed = (
        P(None, "row", "layer", "col"),
        P(None, "row", "layer", "col"),
        P("layer", "row", "col"),
        P("layer", "row", "col"),
        P("layer", "row", "col"),
    )
    sizes = (mesh.shape["row"], mesh.shape["col"], mesh.shape["layer"])
    return jax.shard_map(
        functools.partial(body, sizes), mesh=mesh, in_specs=placed, out_specs=P("layer", "row", "col"),
        check_vma=False,
    )
```
